32 devices in a mesh: fsdp: 16 (over z, x, core), tensor: 2 (over y).
Axes of the slice: x: 2, y: 2, z: 4, core: 2. Of those that a mesh axis runs over, the one named last changes fastest.
Arguments:
- tokens: bfloat16 [16, 1024, 1024], P('fsdp', 'tensor'), may hold values from -6 to 6
- segments: int32 [16, 1024], P('fsdp'), may hold values from 0 to 14, as said below
- attn_gain: bfloat16 [1024], P('fsdp'), may hold values from 0.5 to 1.5
- mlp_gain: bfloat16 [1024], P('fsdp'), may hold values from 0.5 to 1.5
- query_gain: bfloat16 [128], P('fsdp'), may hold values from 0.25 to 1.75
- key_gain: bfloat16 [128], P('fsdp'), may hold values from 0.25 to 1.75
- query_weight: bfloat16 [1024, 2048], P('fsdp', 'tensor'), may hold values from -0.1875 to 0.1875
- key_matrix: bfloat16 [1024, 1024], P('fsdp', 'tensor'), may hold values from -0.1875 to 0.1875
- value_matrix: bfloat16 [1024, 1024], P('fsdp', 'tensor'), may hold values from -0.1875 to 0.1875
- output_weight: bfloat16 [2048, 1024], P('tensor', 'fsdp'), may hold values from -1 to 1
- gate_weight: bfloat16 [1024, 3072], P('fsdp', 'tensor'), may hold values from -0.1875 to 0.1875
- up_weight: bfloat16 [1024, 3072], P('fsdp', 'tensor'), may hold values from -0.1875 to 0.1875
- down_weight: bfloat16 [3072, 1024], P('tensor', 'fsdp'), may hold values from -0.109375 to 0.109375
- cotangent: bfloat16 [16, 1024, 1024], P('fsdp', 'tensor'), may hold values from -6 to 6
Outputs:
- layer_out: bfloat16 [16, 1024, 1024], P('fsdp', 'tensor')
- grad_tokens: float32 [16, 1024, 1024], P('fsdp', 'tensor')
- attn_gain_grad: float32 [1024], P('fsdp')
- mlp_gain_grad: float32 [1024], P('fsdp')
- query_gain_grad: float32 [128], P('fsdp')
- key_gain_grad: float32 [128], P('fsdp')
- query_grad: float32 [1024, 2048], P('fsdp', 'tensor')
- key_grad: float32 [1024, 1024], P('fsdp', 'tensor')
- value_grad: float32 [1024, 1024], P('fsdp', 'tensor')
- output_grad: float32 [2048, 1024], P('tensor', 'fsdp')
- gate_grad: float32 [1024, 3072], P('fsdp', 'tensor')
- up_grad: float32 [1024, 3072], P('fsdp', 'tensor')
- down_grad: float32 [3072, 1024], P('tensor', 'fsdp')
The draws below stay inside these ranges and needn't reach their ends.
Inputs may be any that keep to these rules, and one draw needn't show every extreme that they name: `segments`: numbers the documents of each sequence from 0 upward in order, rising by one at each document start; every document starts at a multiple of 64 tokens.
All inputs are finite; a program needn't handle non-finite values.
Results may differ from the reference program's by a relative error of at most 0.014.
Values may be sent and summed in bfloat16 or wider, within the bound.
A program may use at most 256 MiB of HBM per device.

```python
import jax
import jax.numpy as jnp
from jax import lax

MODEL_WIDTH = 1024
HQ = 16
KEY_VALUE_HEADS = 8
HEAD_SIZE = 128
FF = 3072
SEQ_LEN = 1024
SEQ_DEV = 1
SEQS = 16
N_FSDP = 16
N_TENSOR = 2


def draw_segments(key, part):
    key = jax.random.fold_in(key, 7)
    grain_rows = SEQ_LEN // 16
    cut_draw = jax.random.randint(jax.random.fold_in(key, 1), (SEQS, 15), 0, 2, dtype=jnp.int32)
    cut_spots = jnp.arange(1, 16, dtype=jnp.int32) * grain_rows
    shard_rows = SEQ_LEN // N_TENSOR
    banned = (cut_spots >= shard_rows) & (cut_spots <= SEQ_LEN - shard_rows)
    picked = jax.random.randint(jax.random.fold_in(key, 2), (N_FSDP,), 0, SEQ_DEV, dtype=jnp.int32)
    seq_index = jnp.arange(SEQS, dtype=jnp.int32)
    forced = seq_index == (picked[0] + 1) % SEQ_DEV
    cut_draw = jnp.where(forced[:, None], 1, cut_draw)
    chosen = seq_index % SEQ_DEV == jnp.repeat(picked, SEQ_DEV)
    cut_flags = jnp.where(chosen[:, None] & banned[None, :], 0, cut_draw)
    cut_marks = jnp.zeros((SEQS, SEQ_LEN), jnp.int32).at[:, cut_spots].set(cut_flags)
    return jnp.cumsum(cut_marks, axis=1).astype(jnp.int32)


def shard_levels(stream_key, shape, shards, low, top_value):
    loudness, own = 1.0, jax.random.fold_in(stream_key, 6)
    for dim, shards_of in shards:
        draws = jnp.exp(jax.random.uniform(jax.random.fold_in(own, dim), (shards_of,), jnp.float32, low / len(shards), top_value / len(shards)))
        loudness = loudness * jnp.repeat(draws, shape[dim] // shards_of).reshape([-1 if axis == dim else 1 for axis in range(len(shape))])
    return loudness


def scatter_about(rng, dims, scale, reach, shards=(), held_as=jnp.bfloat16):
    factor_of = shard_levels(rng, dims, shards, -0.22, 0.18) if shards else 1.0
    values = jax.random.normal(rng, dims, jnp.float32) * scale * factor_of
    return jnp.minimum(jnp.maximum(values, -reach), reach).astype(held_as)


def setup_inputs(seed: int = 0) -> dict:
    key_list = jax.random.split(jax.random.key(seed), 15)
    tokens = scatter_about(key_list[0], (SEQS, SEQ_LEN, MODEL_WIDTH), 1.0, 6.0, ((0, 16), (1, 2)))
    segments = draw_segments(jax.random.fold_in(key_list[14], 71), 0)
    attn_gain = jnp.clip(1.0 + 0.1 * jax.random.normal(key_list[2], (MODEL_WIDTH,), jnp.float32), 0.5, 1.5).astype(jnp.bfloat16)
    mlp_gain = jnp.clip(1.0 + 0.1 * jax.random.normal(key_list[3], (MODEL_WIDTH,), jnp.float32), 0.5, 1.5).astype(jnp.bfloat16)
    query_gain = jnp.clip(1.0 + 0.15 * jax.random.normal(key_list[4], (HEAD_SIZE,), jnp.float32), 0.25, 1.75).astype(jnp.bfloat16)
    key_gain = jnp.clip(1.0 + 0.15 * jax.random.normal(key_list[5], (HEAD_SIZE,), jnp.float32), 0.25, 1.75).astype(jnp.bfloat16)
    query_weight = scatter_about(key_list[6], (MODEL_WIDTH, HQ * HEAD_SIZE), MODEL_WIDTH ** -0.5, 0.1875, ((0, 16), (1, 2)))
    key_matrix = scatter_about(key_list[7], (MODEL_WIDTH, KEY_VALUE_HEADS * HEAD_SIZE), MODEL_WIDTH ** -0.5, 0.1875, ((0, 16), (1, 2)))
    value_matrix = scatter_about(key_list[8], (MODEL_WIDTH, KEY_VALUE_HEADS * HEAD_SIZE), MODEL_WIDTH ** -0.5, 0.1875, ((0, 16), (1, 2)))
    output_weight = scatter_about(key_list[9], (HQ * HEAD_SIZE, MODEL_WIDTH), (HQ * HEAD_SIZE // 64) ** -0.5, 1.0, ((0, 2), (1, 16)))
    gate_weight = scatter_about(key_list[10], (MODEL_WIDTH, FF), MODEL_WIDTH ** -0.5, 0.1875, ((0, 16), (1, 2)))
    up_weight = scatter_about(key_list[11], (MODEL_WIDTH, FF), MODEL_WIDTH ** -0.5, 0.1875, ((0, 16), (1, 2)))
    down_weight = scatter_about(key_list[12], (FF, MODEL_WIDTH), FF ** -0.5, 0.109375, ((0, 2), (1, 16)))
    cotangent = scatter_about(key_list[13], (SEQS, SEQ_LEN, MODEL_WIDTH), 1.0, 6.0, ((0, 16), (1, 2)))
    return {"tokens": tokens, "segments": segments, "attn_gain": attn_gain, "mlp_gain": mlp_gain, "query_gain": query_gain, "key_gain": key_gain, "query_weight": query_weight, "key_matrix": key_matrix, "value_matrix": value_matrix, "output_weight": output_weight, "gate_weight": gate_weight, "up_weight": up_weight, "down_weight": down_weight, "cotangent": cotangent}


epsilon = 1e-06
rope_base = 1000000.0

@jax.custom_vjp
def low(v):
    return lax.optimization_barrier(v.astype(jnp.bfloat16)).astype(jnp.float32)

@jax.custom_vjp
def low_back(v):
    return v

def low_keep(v):
    return (low(v), None)

def low_pass(kept, grad):
    return (grad,)

def back_keep(v):
    return (v, None)

def back_low(kept, grad):
    return (low(grad),)
low.defvjp(low_keep, low_pass)
low_back.defvjp(back_keep, back_low)

def positions_of(segment_rows):
    seq_length = segment_rows.shape[-1]
    token_index = jnp.arange(seq_length, dtype=jnp.int32)
    change = jnp.concatenate([jnp.ones(segment_rows.shape[:-1] + (1,), bool), segment_rows[..., 1:] != segment_rows[..., :-1]], axis=-1)
    begins = lax.cummax(jnp.where(change, token_index, 0), axis=segment_rows.ndim - 1)
    return (token_index - begins).astype(jnp.int32)

def rope_tables(positions, width):
    half_width = width // 2
    frequency = rope_base ** (-jnp.arange(half_width, dtype=jnp.float32) * 2.0 / width)
    angles = positions.astype(jnp.float32)[..., None] * frequency
    cosine_table = jnp.cos(angles)
    sine_table = jnp.sin(angles)
    return (jnp.concatenate([cosine_table, cosine_table], -1), jnp.concatenate([sine_table, sine_table], -1))

def rotate(vector, cosine_table, sine_table):
    half_width = vector.shape[-1] // 2
    turned = jnp.concatenate([-vector[..., half_width:], vector[..., :half_width]], -1)
    return vector * cosine_table + turned * sine_table

def rms_norm(vector, gain_vector):
    return vector * lax.rsqrt(lax.optimization_barrier(jnp.mean(vector * vector, axis=-1, keepdims=True)) + epsilon) * gain_vector

def matmul(left_factor, right_factor):
    return jnp.einsum('fta,ay->fty', left_factor, right_factor, precision=lax.Precision.HIGHEST)

def attend(query_seq, key_seq, value_seq, segment_row):
    seq_length, key_heads, head_dim = key_seq.shape
    grouped = query_seq.reshape(seq_length, key_heads, -1, head_dim)
    scores = low_back(jnp.einsum('ikgd,jkd->kgij', grouped, key_seq, precision=lax.Precision.HIGHEST) * head_dim ** (-0.5))
    token_index = jnp.arange(seq_length)
    allowed = (segment_row[:, None] == segment_row[None, :]) & (token_index[None, :] <= token_index[:, None])
    masked = jnp.where(allowed, scores, -1000000000.0)
    row_max = lax.optimization_barrier(jnp.max(masked, -1, keepdims=True))
    exponent = jnp.exp(masked - row_max)
    soft_probs = low(exponent / lax.optimization_barrier(jnp.sum(exponent, -1, keepdims=True)))
    output = jnp.einsum('kgij,jkd->ikgd', soft_probs, value_seq, precision=lax.Precision.HIGHEST)
    return output.reshape(seq_length, -1)

def block_forward(block_in, weight_set, segment_rows):
    attn_gain, mlp_gain, query_gain, key_gain, query_weight, key_matrix, value_matrix, output_weight, gate_weight, up_weight, down_weight = weight_set
    seq_count, seq_length, width = block_in.shape
    head_dim = query_gain.shape[0]
    hidden = low(rms_norm(block_in, attn_gain))
    query_raw = low_back(matmul(hidden, query_weight)).reshape(seq_count, seq_length, -1, head_dim)
    unrotated_key = low_back(matmul(hidden, key_matrix)).reshape(seq_count, seq_length, -1, head_dim)
    value = low(low_back(matmul(hidden, value_matrix))).reshape(seq_count, seq_length, -1, head_dim)
    cosine_table, sine_table = rope_tables(positions_of(segment_rows), head_dim)
    cosine_table = cosine_table[:, :, None, :]
    sine_table = sine_table[:, :, None, :]
    query_rot = low(low_back(rotate(rms_norm(query_raw, query_gain), cosine_table, sine_table)))
    key_rot = low(low_back(rotate(rms_norm(unrotated_key, key_gain), cosine_table, sine_table)))
    checked = jax.checkpoint(attend)
    attended_rows = lax.map(lambda members: checked(*members), (query_rot, key_rot, value, segment_rows))
    attended_rows = low(low_back(attended_rows))
    middle = block_in + low_back(matmul(attended_rows, output_weight))
    second = low(rms_norm(middle, mlp_gain))
    gate_value = low_back(matmul(second, gate_weight))
    up_projected = low_back(matmul(second, up_weight))
    active_product = low(jax.nn.silu(gate_value) * up_projected)
    return middle + low_back(matmul(active_product, down_weight))

def reference(tokens, segments, attn_gain, mlp_gain, query_gain, key_gain, query_weight, key_matrix, value_matrix, output_weight, gate_weight, up_weight, down_weight, cotangent):
    weight_set = tuple((member.astype(jnp.float32) for member in (attn_gain, mlp_gain, query_gain, key_gain, query_weight, key_matrix, value_matrix, output_weight, gate_weight, up_weight, down_weight)))
    inputs_all = tokens.astype(jnp.float32).reshape(N_FSDP, SEQ_DEV, SEQ_LEN, MODEL_WIDTH)
    segment_all = segments.reshape(N_FSDP, SEQ_DEV, SEQ_LEN)
    cotangent_all = cotangent.astype(jnp.float32).reshape(N_FSDP, SEQ_DEV, SEQ_LEN, MODEL_WIDTH)

    def one_block(grad_total, members):
        block_in, block_segments, block_cotangent = members
        block_out, pullback = jax.vjp(lambda inputs_x, weights_w: block_forward(inputs_x, weights_w, block_segments), block_in, weight_set)
        grad_input, grad_weights = pullback(block_cotangent)
        grad_total = jax.tree.map(jnp.add, grad_total, grad_weights)
        return (grad_total, (block_out.astype(jnp.bfloat16), grad_input))
    zero_grads = jax.tree.map(jnp.zeros_like, weight_set)
    grad_total, (outputs_all, grads_all) = lax.scan(one_block, zero_grads, (inputs_all, segment_all, cotangent_all))
    layer_out = outputs_all.reshape(SEQS, SEQ_LEN, MODEL_WIDTH)
    grad_tokens = grads_all.reshape(SEQS, SEQ_LEN, MODEL_WIDTH)
    return (layer_out, grad_tokens, grad_total[0], grad_total[1], grad_total[2], grad_total[3], grad_total[4], grad_total[5], grad_total[6], grad_total[7], grad_total[8], grad_total[9], grad_total[10])
```

```python
import functools

import jax
import jax.numpy as jnp
from jax import lax
from jax.experimental import pallas as pl
from jax.experimental.pallas import tpu as pltpu
from jax.sharding import PartitionSpec as P

epsilon = 1e-06
rope_base = 1000000.0
LANES = 128
BF = jnp.bfloat16
F32 = jnp.float32


def starts_of(segment_rows):
    seq_length = segment_rows.shape[-1]
    token_index = jnp.arange(seq_length, dtype=jnp.int32)
    change = jnp.concatenate(
        [
            jnp.ones(segment_rows.shape[:-1] + (1,), bool),
            segment_rows[..., 1:] != segment_rows[..., :-1],
        ],
        axis=-1,
    )
    return lax.cummax(jnp.where(change, token_index, 0), axis=segment_rows.ndim - 1)


def rope_tables(positions, width):
    half_width = width // 2
    frequency = rope_base ** (-jnp.arange(half_width, dtype=F32) * 2.0 / width)
    angles = positions.astype(F32)[..., None] * frequency
    cosine_table = jnp.cos(angles)
    sine_table = jnp.sin(angles)
    return (
        jnp.concatenate([cosine_table, cosine_table], -1),
        jnp.concatenate([-sine_table, sine_table], -1),
    )


def scale_of(vector):
    return lax.rsqrt(jnp.mean(vector * vector, axis=-1, keepdims=True) + epsilon)


def nt(left, right):
    return lax.dot_general(left, right, (((1,), (1,)), ((), ())), preferred_element_type=F32)


def nn(left, right):
    return jnp.dot(left, right, preferred_element_type=F32)


def tn(left, right):
    return lax.dot_general(left, right, (((0,), (0,)), ((), ())), preferred_element_type=F32)


def turn(vector):
    return pltpu.roll(vector, vector.shape[1] // 2, 1)


def prepared(raw, gain, cosine, sine):
    inverse = scale_of(raw)
    normed = raw * inverse
    gained = normed * gain
    return (gained * cosine + turn(gained) * sine).astype(BF), normed, inverse


def scores_block(key_part, query_part, starts, first_row, scale):
    scores = nt(key_part, query_part) * scale
    key_index = lax.broadcasted_iota(jnp.int32, scores.shape, 0)
    query_index = lax.broadcasted_iota(jnp.int32, scores.shape, 1) + first_row
    allowed = (key_index <= query_index) & (key_index >= starts)
    return jnp.where(allowed, scores, -1000000000.0)


def soft_block(scores):
    exponent = jnp.exp(scores - jnp.max(scores, axis=0, keepdims=True))
    return exponent * (1.0 / jnp.sum(exponent, axis=0, keepdims=True))


def forward_kernel(
    group, block, q_ref, k_ref, v_ref, cos_ref, sin_ref, starts_ref, qg_ref, kg_ref, out_ref
):
    seq_length, head_dim = k_ref.shape
    scale = head_dim**-0.5
    cosine, sine = cos_ref[...], sin_ref[...]
    key_rot, _, _ = prepared(k_ref[...], kg_ref[...], cosine, sine)
    value_turned = v_ref[...].T.astype(BF)
    for head in range(group):
        columns = slice(head * head_dim, (head + 1) * head_dim)
        query_rot, _, _ = prepared(q_ref[:, columns], qg_ref[...], cosine, sine)
        for first in range(0, seq_length, block):
            last = first + block
            scores = scores_block(
                key_rot[:last], query_rot[first:last], starts_ref[:, first:last], first, scale
            )
            probs = soft_block(scores).astype(BF)
            out_ref[first:last, columns] = nn(value_turned[:, :last], probs).T.astype(BF)


def backward_kernel(
    group,
    block,
    q_ref,
    k_ref,
    v_ref,
    grad_ref,
    cos_ref,
    sin_ref,
    starts_ref,
    qg_ref,
    kg_ref,
    dq_ref,
    dk_ref,
    dv_ref,
    gains_ref,
    key_total,
    value_total,
    query_total,
):
    seq_length, head_dim = k_ref.shape
    scale = head_dim**-0.5
    cosine, sine = cos_ref[...], sin_ref[...]
    key_gain, query_gain = kg_ref[...], qg_ref[...]
    key_rot, key_normed, key_inverse = prepared(k_ref[...], key_gain, cosine, sine)
    key_turned = key_rot.astype(F32).T.astype(BF)
    value = v_ref[...].astype(BF)

    def norm_back(rounded, normed, inverse, gain):
        gradient = rounded.astype(BF).astype(F32)
        gradient = gradient * cosine - turn(gradient) * sine
        gain_grad = jnp.sum(gradient * normed, axis=0, keepdims=True)
        shaped = gradient * gain
        inner = jnp.mean(shaped * normed, axis=-1, keepdims=True)
        return (inverse * (shaped - normed * inner)).astype(BF), gain_grad

    key_total[...] = jnp.zeros_like(key_total)
    value_total[...] = jnp.zeros_like(value_total)
    gain_total = jnp.zeros((1, head_dim), F32)
    for head in range(group):
        columns = slice(head * head_dim, (head + 1) * head_dim)
        query_rot, query_normed, query_inverse = prepared(
            q_ref[:, columns], query_gain, cosine, sine
        )
        for first in range(0, seq_length, block):
            last = first + block
            query_part = query_rot[first:last]
            grad_part = grad_ref[first:last, columns]
            probs = soft_block(
                scores_block(key_rot[:last], query_part, starts_ref[:, first:last], first, scale)
            )
            grad_probs = nt(value[:last], grad_part)
            delta = jnp.sum(grad_probs * probs, axis=0, keepdims=True)
            score_grad = (probs * (grad_probs - delta)).astype(BF)
            value_total[:last, :] += nn(probs.astype(BF), grad_part)
            key_total[:last, :] += nn(score_grad, query_part)
            query_total[first:last, :] = nn(key_turned[:, :last], score_grad).T
        query_back, gain_part = norm_back(
            query_total[...] * scale, query_normed, query_inverse, query_gain
        )
        dq_ref[:, columns] = query_back
        gain_total = gain_total + gain_part
    key_back, key_gain_part = norm_back(key_total[...] * scale, key_normed, key_inverse, key_gain)
    dk_ref[...] = key_back
    dv_ref[...] = value_total[...].astype(BF)
    gains_ref[0:1, :] = gain_total
    gains_ref[1:2, :] = key_gain_part


def attention_specs(seq_length, query_width, key_width, head_dim):
    key_heads = key_width // head_dim
    group = query_width // key_width
    key_base = query_width // head_dim
    value_base = key_base + key_heads
    raw = [
        pl.BlockSpec((seq_length, group * head_dim), lambda s, h: (s, h)),
        pl.BlockSpec((seq_length, head_dim), lambda s, h: (s, key_base + h)),
        pl.BlockSpec((seq_length, head_dim), lambda s, h: (s, value_base + h)),
    ]
    tables = [
        pl.BlockSpec((seq_length, head_dim), lambda s, h: (s, 0)),
        pl.BlockSpec((seq_length, head_dim), lambda s, h: (s, 0)),
        pl.BlockSpec((None, 1, seq_length), lambda s, h: (s, 0, 0)),
        pl.BlockSpec((1, head_dim), lambda s, h: (0, 0)),
        pl.BlockSpec((1, head_dim), lambda s, h: (0, 0)),
    ]
    return raw, tables, group, key_heads


def attend_forward(qkv, tables, seq_count, query_width, key_width):
    seq_length = qkv.shape[0] // seq_count
    head_dim = tables[0].shape[-1]
    raw_specs, table_specs, group, key_heads = attention_specs(
        seq_length, query_width, key_width, head_dim
    )
    block = min(256, seq_length)
    return pl.pallas_call(
        functools.partial(forward_kernel, group, block),
        grid=(seq_count, key_heads),
        in_specs=raw_specs + table_specs,
        out_specs=pl.BlockSpec((seq_length, group * head_dim), lambda s, h: (s, h)),
        out_shape=jax.ShapeDtypeStruct((qkv.shape[0], query_width), BF),
        compiler_params=pltpu.CompilerParams(vmem_limit_bytes=40 * 2**20),
        cost_estimate=pl.CostEstimate(
            flops=3 * seq_count * seq_length * seq_length * query_width,
            bytes_accessed=qkv.size * 4 + qkv.shape[0] * query_width * 2,
            transcendentals=seq_count * seq_length * seq_length * query_width // head_dim,
        ),
    )(qkv, qkv, qkv, *tables)


def attend_backward(qkv, grad_mixed, tables, seq_count, query_width, key_width):
    seq_length = qkv.shape[0] // seq_count
    head_dim = tables[0].shape[-1]
    raw_specs, table_specs, group, key_heads = attention_specs(
        seq_length, query_width, key_width, head_dim
    )
    block = min(256, seq_length)
    rows = qkv.shape[0]
    wide = pl.BlockSpec((seq_length, group * head_dim), lambda s, h: (s, h))
    narrow = pl.BlockSpec((seq_length, head_dim), lambda s, h: (s, h))
    return pl.pallas_call(
        functools.partial(backward_kernel, group, block),
        grid=(seq_count, key_heads),
        in_specs=raw_specs + [wide] + table_specs,
        out_specs=[
            wide,
            narrow,
            narrow,
            pl.BlockSpec((None, None, 2, head_dim), lambda s, h: (s, h, 0, 0)),
        ],
        out_shape=[
            jax.ShapeDtypeStruct((rows, query_width), BF),
            jax.ShapeDtypeStruct((rows, key_width), BF),
            jax.ShapeDtypeStruct((rows, key_width), BF),
            jax.ShapeDtypeStruct((seq_count, key_heads, 2, head_dim), F32),
        ],
        scratch_shapes=[pltpu.VMEM((seq_length, head_dim), F32)] * 3,
        compiler_params=pltpu.CompilerParams(vmem_limit_bytes=48 * 2**20),
        cost_estimate=pl.CostEstimate(
            flops=7 * seq_count * seq_length * seq_length * query_width,
            bytes_accessed=qkv.size * 6 + rows * query_width * 2,
            transcendentals=seq_count * seq_length * seq_length * query_width // head_dim,
        ),
    )(qkv, qkv, qkv, grad_mixed, *tables)


def local(
    n_tensor,
    tokens,
    segments,
    attn_gain,
    mlp_gain,
    query_gain,
    key_gain,
    query_weight,
    key_matrix,
    value_matrix,
    output_weight,
    gate_weight,
    up_weight,
    down_weight,
    cotangent,
):
    seq_count, local_rows, width = tokens.shape
    seq_length = segments.shape[1]
    shard_rows = attn_gain.shape[0]
    head_rows = query_gain.shape[0]
    query_width = query_weight.shape[1]
    key_width = key_matrix.shape[1]
    hidden_units = gate_weight.shape[1]
    qkv_width = query_width + 2 * key_width
    me = lax.axis_index("tensor")
    swap = [(0, 1), (1, 0)]

    def rows_all(member):
        if n_tensor == 2:
            other = lax.ppermute(member, "tensor", swap)
            return jnp.concatenate(
                [jnp.where(me == 0, member, other), jnp.where(me == 0, other, member)], axis=1
            )
        return lax.all_gather(member, "tensor", axis=1, tiled=True)

    def rows_sum(member):
        member = member.reshape(seq_count, seq_length, width)
        if n_tensor == 2:
            lower, upper = member[:, :local_rows], member[:, local_rows:]
            sent = jnp.where(me == 0, upper, lower).astype(BF)
            kept = jnp.where(me == 0, lower, upper)
            return kept + lax.ppermute(sent, "tensor", swap).astype(F32)
        return lax.psum_scatter(member, "tensor", scatter_dimension=1, tiled=True)

    def flat(member):
        return member.reshape(seq_count * seq_length, -1)

    def column(vector):
        return jnp.pad(vector[:, None], ((0, shard_rows - vector.shape[0]), (0, 0)))

    gain_columns = jnp.concatenate(
        [column(member) for member in (attn_gain, mlp_gain, query_gain, key_gain)], axis=1
    )
    gain_columns = jnp.pad(gain_columns, ((0, 0), (0, LANES - 4)))
    first_shard = jnp.concatenate(
        [query_weight, key_matrix, value_matrix, output_weight.T, gain_columns], axis=1
    )
    second_shard = jnp.concatenate([gate_weight, up_weight, down_weight.T], axis=1)
    first_all = lax.all_gather(first_shard, "fsdp", axis=0, tiled=True)
    second_all = lax.all_gather(second_shard, "fsdp", axis=0, tiled=True)
    weight_qkv = first_all[:, :qkv_width]
    weight_out = first_all[:, qkv_width : qkv_width + query_width]
    gains = first_all[:, qkv_width + query_width :].astype(F32)
    gain_attn, gain_mlp = gains[:, 0], gains[:, 1]
    split_gains = gains.reshape(-1, shard_rows, LANES)[:, :head_rows]
    gain_query = split_gains[:, :, 2].reshape(1, -1)
    gain_key = split_gains[:, :, 3].reshape(1, -1)
    weight_gate = second_all[:, :hidden_units]
    weight_up = second_all[:, hidden_units : 2 * hidden_units]
    weight_down = second_all[:, 2 * hidden_units :]
    head_dim = gain_query.shape[1]

    tokens_all = rows_all(tokens)
    cotangent_all = flat(rows_all(cotangent))
    starts = starts_of(segments)
    positions = jnp.arange(seq_length, dtype=jnp.int32) - starts
    cosine_table, sine_table = rope_tables(positions, head_dim)
    tables = (
        flat(cosine_table),
        flat(sine_table),
        starts.reshape(seq_count, 1, seq_length),
        gain_query,
        gain_key,
    )

    source = tokens.astype(F32)
    inverse_one = scale_of(source)
    normed_one = source * inverse_one
    source_all = flat(tokens_all.astype(F32))
    normed_all = source_all * scale_of(source_all)
    first_hidden = (normed_all * gain_attn).astype(BF)
    qkv = nn(first_hidden, weight_qkv)
    attended = attend_forward(qkv, tables, seq_count, query_width, key_width)
    middle = source + rows_sum(nt(attended, weight_out))
    inverse_two = scale_of(middle)
    normed_two = middle * inverse_two
    second_hidden = flat(rows_all((normed_two * gain_mlp).astype(BF)))

    gate_value = nn(second_hidden, weight_gate)
    up_projected = nn(second_hidden, weight_up)
    sigmoid_gate = jax.nn.sigmoid(gate_value)
    silu_gate = gate_value * sigmoid_gate
    active = (silu_gate * up_projected).astype(BF)
    active_gradient = nn(cotangent_all, weight_down)
    gate_rows = (
        active_gradient * up_projected * (sigmoid_gate * (1.0 + gate_value * (1.0 - sigmoid_gate)))
    ).astype(BF)
    up_rows = (active_gradient * silu_gate).astype(BF)
    hidden_two_part = nt(gate_rows, weight_gate) + nt(up_rows, weight_up)
    dsecond = rows_sum(hidden_two_part)
    layer_out = (middle + rows_sum(nt(active, weight_down))).astype(BF)

    mlp_gain_part = jnp.sum(dsecond * normed_two, axis=(0, 1))
    shaped = dsecond * gain_mlp
    back_two = inverse_two * (
        shaped - normed_two * jnp.mean(shaped * normed_two, axis=-1, keepdims=True)
    )
    grad_middle = cotangent.astype(F32) + back_two

    mlp_grads = jnp.concatenate(
        [
            tn(second_hidden, gate_rows).astype(BF),
            tn(second_hidden, up_rows).astype(BF),
            tn(cotangent_all, active).astype(BF),
        ],
        axis=1,
    )
    mlp_sums = lax.psum_scatter(mlp_grads, "fsdp", scatter_dimension=0, tiled=True)

    attention_gradient = flat(rows_all(grad_middle.astype(BF)))
    grad_mixed = nn(attention_gradient, weight_out).astype(BF)
    query_back, key_back, value_back, head_gains = attend_backward(
        qkv, grad_mixed, tables, seq_count, query_width, key_width
    )
    qkv_back = jnp.concatenate([query_back, key_back, value_back], axis=1)
    hidden_one_part = nt(qkv_back, weight_qkv)
    attn_gain_part = jnp.sum(hidden_one_part * normed_all, axis=0)
    head_gains = jnp.sum(head_gains, axis=(0, 1))

    def spread(vector):
        split = vector.reshape(-1, head_rows)
        return jnp.pad(split, ((0, 0), (0, shard_rows - head_rows))).reshape(-1)

    gain_parts = jnp.stack(
        [attn_gain_part, mlp_gain_part, spread(head_gains[0]), spread(head_gains[1])], axis=1
    )
    attention_grads = jnp.concatenate(
        [
            tn(first_hidden, qkv_back).astype(BF),
            tn(attention_gradient, attended).astype(BF),
            jnp.pad(gain_parts, ((0, 0), (0, LANES - 4))).astype(BF),
        ],
        axis=1,
    )
    attention_sums = lax.psum_scatter(
        attention_grads, "fsdp", scatter_dimension=0, tiled=True
    ).astype(F32)
    gain_sums = lax.psum(attention_sums[:, qkv_width + query_width :], "tensor") if (
        n_tensor != 2
    ) else attention_sums[:, qkv_width + query_width :] + lax.ppermute(
        attention_sums[:, qkv_width + query_width :], "tensor", swap
    )

    dhidden = rows_sum(hidden_one_part)
    shaped = dhidden * gain_attn
    back_one = inverse_one * (
        shaped - normed_one * jnp.mean(shaped * normed_one, axis=-1, keepdims=True)
    )
    grad_tokens = grad_middle + back_one
    mlp_sums = mlp_sums.astype(F32)
    return (
        layer_out,
        grad_tokens,
        gain_sums[:, 0],
        gain_sums[:, 1],
        gain_sums[:head_rows, 2],
        gain_sums[:head_rows, 3],
        attention_sums[:, :query_width],
        attention_sums[:, query_width : query_width + key_width],
        attention_sums[:, query_width + key_width : qkv_width],
        attention_sums[:, qkv_width : qkv_width + query_width].T,
        mlp_sums[:, :hidden_units],
        mlp_sums[:, hidden_units : 2 * hidden_units],
        mlp_sums[:, 2 * hidden_units :].T,
    )


def solution(mesh):
    split = P("fsdp", "tensor")
    turned = P("tensor", "fsdp")
    rows = P("fsdp", "tensor", None)
    vector = P("fsdp")
    in_specs = (rows, P("fsdp", None), vector, vector, vector, vector)
    in_specs = in_specs + (split, split, split, turned, split, split, turned, rows)
    out_specs = (rows, rows, vector, vector, vector, vector)
    out_specs = out_specs + (split, split, split, turned, split, split, turned)
    return jax.shard_map(
        functools.partial(local, mesh.shape["tensor"]),
        mesh=mesh,
        in_specs=in_specs,
        out_specs=out_specs,
        check_vma=False,
    )
```

```python
import functools

import jax
import jax.numpy as jnp
from jax import lax
from jax.experimental import pallas as pl
from jax.experimental.pallas import tpu as pltpu
from jax.sharding import PartitionSpec as P

epsilon = 1e-06
rope_base = 1000000.0
LANES = 128
BF = jnp.bfloat16
F32 = jnp.float32


def starts_of(segment_rows):
    seq_length = segment_rows.shape[-1]
    token_index = jnp.arange(seq_length, dtype=jnp.int32)
    change = jnp.concatenate(
        [
            jnp.ones(segment_rows.shape[:-1] + (1,), bool),
            segment_rows[..., 1:] != segment_rows[..., :-1],
        ],
        axis=-1,
    )
    return lax.cummax(jnp.where(change, token_index, 0), axis=segment_rows.ndim - 1)


def rope_tables(positions, width):
    half_width = width // 2
    frequency = rope_base ** (-jnp.arange(half_width, dtype=F32) * 2.0 / width)
    angles = positions.astype(F32)[..., None] * frequency
    cosine_table = jnp.cos(angles)
    sine_table = jnp.sin(angles)
    return (
        jnp.concatenate([cosine_table, cosine_table], -1),
        jnp.concatenate([-sine_table, sine_table], -1),
    )


def scale_of(vector):
    return lax.rsqrt(jnp.mean(vector * vector, axis=-1, keepdims=True) + epsilon)


def nt(left, right):
    return lax.dot_general(left, right, (((1,), (1,)), ((), ())), preferred_element_type=F32)


def nn(left, right):
    return jnp.dot(left, right, preferred_element_type=F32)


def tn(left, right):
    return lax.dot_general(left, right, (((0,), (0,)), ((), ())), preferred_element_type=F32)


def turn(vector):
    return pltpu.roll(vector, vector.shape[1] // 2, 1)


def prepared(raw, gain, cosine, sine):
    inverse = scale_of(raw)
    normed = raw * inverse
    gained = normed * gain
    return (gained * cosine + turn(gained) * sine).astype(BF), normed, inverse


def scores_block(key_part, query_part, starts, key_first, query_first, scale):
    scores = nt(key_part, query_part) * scale
    key_index = lax.broadcasted_iota(jnp.int32, scores.shape, 0) + key_first
    query_index = lax.broadcasted_iota(jnp.int32, scores.shape, 1) + query_first
    allowed = (key_index <= query_index) & (key_index >= starts)
    return jnp.where(allowed, scores, -1000000000.0)


def soft_block(scores):
    exponent = jnp.exp(scores - jnp.max(scores, axis=0, keepdims=True))
    return exponent * (1.0 / jnp.sum(exponent, axis=0, keepdims=True))


def for_windows(begins_ref, block, grain, seq_length, body):
    sequence = pl.program_id(0)
    for first in range(0, seq_length, block):
        tile = begins_ref[sequence, first // block] // grain
        for lower in range(0, first + 1, grain):

            @pl.when(tile == lower // grain)
            def _(lower=lower, first=first):
                body(lower, first, first + block)


def forward_kernel(
    group,
    block,
    grain,
    begins_ref,
    q_ref,
    k_ref,
    v_ref,
    cos_ref,
    sin_ref,
    starts_ref,
    qg_ref,
    kg_ref,
    out_ref,
    key_rot,
    value_turned,
    query_rot,
):
    seq_length, head_dim = k_ref.shape
    scale = head_dim**-0.5
    cosine, sine = cos_ref[...], sin_ref[...]

    @pl.when(pl.program_id(2) == 0)
    def _():
        key_rot[...] = prepared(k_ref[...], kg_ref[...], cosine, sine)[0]
        value_turned[...] = v_ref[...].T.astype(BF)

    query_rot[...] = prepared(q_ref[...], qg_ref[...], cosine, sine)[0]

    def body(lower, first, last):
        scores = scores_block(
            key_rot[lower:last, :],
            query_rot[first:last, :],
            starts_ref[:, first:last],
            lower,
            first,
            scale,
        )
        probs = soft_block(scores).astype(BF)
        out_ref[first:last, :] = nn(value_turned[:, lower:last], probs).T.astype(BF)

    for_windows(begins_ref, block, grain, seq_length, body)


def backward_kernel(
    group,
    block,
    grain,
    begins_ref,
    q_ref,
    k_ref,
    v_ref,
    grad_ref,
    cos_ref,
    sin_ref,
    starts_ref,
    qg_ref,
    kg_ref,
    dq_ref,
    dk_ref,
    dv_ref,
    gains_ref,
    key_total,
    value_total,
    query_total,
    key_rot,
    key_turned,
    value,
    query_rot,
):
    seq_length, head_dim = k_ref.shape
    scale = head_dim**-0.5
    cosine, sine = cos_ref[...], sin_ref[...]
    key_gain, query_gain = kg_ref[...], qg_ref[...]

    @pl.when(pl.program_id(2) == 0)
    def _():
        rotated = prepared(k_ref[...], key_gain, cosine, sine)[0]
        key_rot[...] = rotated
        key_turned[...] = rotated.astype(F32).T.astype(BF)
        value[...] = v_ref[...].astype(BF)
        key_total[...] = jnp.zeros_like(key_total)
        value_total[...] = jnp.zeros_like(value_total)

    query_rotated, query_normed, query_inverse = prepared(q_ref[...], query_gain, cosine, sine)
    query_rot[...] = query_rotated

    def norm_back(rounded, normed, inverse, gain):
        gradient = rounded.astype(BF).astype(F32)
        gradient = gradient * cosine - turn(gradient) * sine
        gain_grad = jnp.sum(gradient * normed, axis=0, keepdims=True)
        shaped = gradient * gain
        inner = jnp.mean(shaped * normed, axis=-1, keepdims=True)
        return (inverse * (shaped - normed * inner)).astype(BF), gain_grad

    def body(lower, first, last):
        query_part = query_rot[first:last, :]
        grad_part = grad_ref[first:last, :]
        probs = soft_block(
            scores_block(
                key_rot[lower:last, :],
                query_part,
                starts_ref[:, first:last],
                lower,
                first,
                scale,
            )
        )
        grad_probs = nt(value[lower:last, :], grad_part)
        delta = jnp.sum(grad_probs * probs, axis=0, keepdims=True)
        score_grad = (probs * (grad_probs - delta)).astype(BF)
        value_total[lower:last, :] += nn(probs.astype(BF), grad_part)
        key_total[lower:last, :] += nn(score_grad, query_part)
        query_total[first:last, :] = nn(key_turned[:, lower:last], score_grad).T

    for_windows(begins_ref, block, grain, seq_length, body)

    query_back, gain_part = norm_back(
        query_total[...] * scale, query_normed, query_inverse, query_gain
    )
    dq_ref[...] = query_back
    gains_ref[0:1, :] = gain_part
    gains_ref[1:2, :] = jnp.zeros_like(gain_part)

    @pl.when(pl.program_id(2) == group - 1)
    def _():
        _, key_normed, key_inverse = prepared(k_ref[...], key_gain, cosine, sine)
        key_back, key_gain_part = norm_back(
            key_total[...] * scale, key_normed, key_inverse, key_gain
        )
        dk_ref[...] = key_back
        dv_ref[...] = value_total[...].astype(BF)
        gains_ref[1:2, :] = key_gain_part


def attention_specs(seq_length, query_width, key_width, head_dim):
    key_heads = key_width // head_dim
    group = query_width // key_width
    key_base = query_width // head_dim
    value_base = key_base + key_heads
    wide = pl.BlockSpec((seq_length, head_dim), lambda s, h, g, b: (s, h * group + g))
    narrow = pl.BlockSpec((seq_length, head_dim), lambda s, h, g, b: (s, h))
    raw = [
        wide,
        pl.BlockSpec((seq_length, head_dim), lambda s, h, g, b: (s, key_base + h)),
        pl.BlockSpec((seq_length, head_dim), lambda s, h, g, b: (s, value_base + h)),
    ]
    tables = [
        pl.BlockSpec((seq_length, head_dim), lambda s, h, g, b: (s, 0)),
        pl.BlockSpec((seq_length, head_dim), lambda s, h, g, b: (s, 0)),
        pl.BlockSpec((None, 1, seq_length), lambda s, h, g, b: (s, 0, 0)),
        pl.BlockSpec((1, head_dim), lambda s, h, g, b: (0, 0)),
        pl.BlockSpec((1, head_dim), lambda s, h, g, b: (0, 0)),
    ]
    return raw, tables, wide, narrow, group, key_heads


def attention_tiles(seq_length):
    return min(256, seq_length), min(128, seq_length)


def attend_forward(qkv, tables, seq_count, query_width, key_width):
    seq_length = qkv.shape[0] // seq_count
    head_dim = tables[0].shape[-1]
    raw_specs, table_specs, wide, _, group, key_heads = attention_specs(
        seq_length, query_width, key_width, head_dim
    )
    block, grain = attention_tiles(seq_length)
    begins = tables[2][:, 0, ::block]
    return pl.pallas_call(
        functools.partial(forward_kernel, group, block, grain),
        grid_spec=pltpu.PrefetchScalarGridSpec(
            num_scalar_prefetch=1,
            grid=(seq_count, key_heads, group),
            in_specs=raw_specs + table_specs,
            out_specs=wide,
            scratch_shapes=[
                pltpu.VMEM((seq_length, head_dim), BF),
                pltpu.VMEM((head_dim, seq_length), BF),
                pltpu.VMEM((seq_length, head_dim), BF),
            ],
        ),
        out_shape=jax.ShapeDtypeStruct((qkv.shape[0], query_width), BF),
        compiler_params=pltpu.CompilerParams(vmem_limit_bytes=32 * 2**20),
        cost_estimate=pl.CostEstimate(
            flops=2 * seq_count * seq_length * seq_length * query_width,
            bytes_accessed=qkv.size * 4 + qkv.shape[0] * query_width * 2,
            transcendentals=seq_count * seq_length * seq_length * query_width // head_dim,
        ),
    )(begins, qkv, qkv, qkv, *tables)


def attend_backward(qkv, grad_mixed, tables, seq_count, query_width, key_width):
    seq_length = qkv.shape[0] // seq_count
    head_dim = tables[0].shape[-1]
    raw_specs, table_specs, wide, narrow, group, key_heads = attention_specs(
        seq_length, query_width, key_width, head_dim
    )
    block, grain = attention_tiles(seq_length)
    begins = tables[2][:, 0, ::block]
    rows = qkv.shape[0]
    total = pltpu.VMEM((seq_length, head_dim), F32)
    part = pltpu.VMEM((seq_length, head_dim), BF)
    return pl.pallas_call(
        functools.partial(backward_kernel, group, block, grain),
        grid_spec=pltpu.PrefetchScalarGridSpec(
            num_scalar_prefetch=1,
            grid=(seq_count, key_heads, group),
            in_specs=raw_specs + [wide] + table_specs,
            out_specs=[
                wide,
                narrow,
                narrow,
                pl.BlockSpec(
                    (None, None, 2, head_dim), lambda s, h, g, b: (s, h * group + g, 0, 0)
                ),
            ],
            scratch_shapes=[total, total, total, part]
            + [pltpu.VMEM((head_dim, seq_length), BF), part, part],
        ),
        out_shape=[
            jax.ShapeDtypeStruct((rows, query_width), BF),
            jax.ShapeDtypeStruct((rows, key_width), BF),
            jax.ShapeDtypeStruct((rows, key_width), BF),
            jax.ShapeDtypeStruct((seq_count, key_heads * group, 2, head_dim), F32),
        ],
        compiler_params=pltpu.CompilerParams(vmem_limit_bytes=32 * 2**20),
        cost_estimate=pl.CostEstimate(
            flops=5 * seq_count * seq_length * seq_length * query_width,
            bytes_accessed=qkv.size * 6 + rows * query_width * 2,
            transcendentals=seq_count * seq_length * seq_length * query_width // head_dim,
        ),
    )(begins, qkv, qkv, qkv, grad_mixed, *tables)


def local(
    n_tensor,
    tokens,
    segments,
    attn_gain,
    mlp_gain,
    query_gain,
    key_gain,
    query_weight,
    key_matrix,
    value_matrix,
    output_weight,
    gate_weight,
    up_weight,
    down_weight,
    cotangent,
):
    seq_count, local_rows, width = tokens.shape
    seq_length = segments.shape[1]
    shard_rows = attn_gain.shape[0]
    head_rows = query_gain.shape[0]
    query_width = query_weight.shape[1]
    key_width = key_matrix.shape[1]
    hidden_units = gate_weight.shape[1]
    qkv_width = query_width + 2 * key_width
    me = lax.axis_index("tensor")
    swap = [(0, 1), (1, 0)]

    def rows_all(member):
        if n_tensor == 2:
            other = lax.ppermute(member, "tensor", swap)
            return jnp.concatenate(
                [jnp.where(me == 0, member, other), jnp.where(me == 0, other, member)], axis=1
            )
        return lax.all_gather(member, "tensor", axis=1, tiled=True)

    def rows_sum(member):
        member = member.reshape(seq_count, seq_length, width)
        if n_tensor == 2:
            lower, upper = member[:, :local_rows], member[:, local_rows:]
            sent = jnp.where(me == 0, upper, lower).astype(BF)
            kept = jnp.where(me == 0, lower, upper)
            return kept + lax.ppermute(sent, "tensor", swap).astype(F32)
        return lax.psum_scatter(member, "tensor", scatter_dimension=1, tiled=True)

    def sum_shards(member):
        return lax.psum_scatter(member, "fsdp", scatter_dimension=0, tiled=True)

    def flat(member):
        return member.reshape(seq_count * seq_length, -1)

    def column(vector):
        return jnp.pad(vector[:, None], ((0, shard_rows - vector.shape[0]), (0, 0)))

    gain_columns = jnp.concatenate(
        [column(member) for member in (attn_gain, mlp_gain, query_gain, key_gain)], axis=1
    )
    gain_columns = jnp.pad(gain_columns, ((0, 0), (0, LANES - 4)))
    first_shard = jnp.concatenate(
        [query_weight, key_matrix, value_matrix, output_weight.T, gain_columns], axis=1
    )
    second_shard = jnp.concatenate([gate_weight, up_weight, down_weight.T], axis=1)
    first_all = lax.all_gather(first_shard, "fsdp", axis=0, tiled=True)
    second_all = lax.all_gather(second_shard, "fsdp", axis=0, tiled=True)
    weight_qkv = first_all[:, :qkv_width]
    weight_out = first_all[:, qkv_width : qkv_width + query_width]
    gains = first_all[:, qkv_width + query_width :].astype(F32)
    gain_attn, gain_mlp = gains[:, 0], gains[:, 1]
    split_gains = gains.reshape(-1, shard_rows, LANES)[:, :head_rows]
    gain_query = split_gains[:, :, 2].reshape(1, -1)
    gain_key = split_gains[:, :, 3].reshape(1, -1)
    weight_gate = second_all[:, :hidden_units]
    weight_up = second_all[:, hidden_units : 2 * hidden_units]
    weight_down = second_all[:, 2 * hidden_units :]
    head_dim = gain_query.shape[1]

    tokens_all, cotangent_all = lax.optimization_barrier((rows_all(tokens), rows_all(cotangent)))
    cotangent_all = flat(cotangent_all)
    starts = starts_of(segments)
    positions = jnp.arange(seq_length, dtype=jnp.int32) - starts
    cosine_table, sine_table = rope_tables(positions, head_dim)
    tables = (
        flat(cosine_table),
        flat(sine_table),
        starts.reshape(seq_count, 1, seq_length),
        gain_query,
        gain_key,
    )

    source = tokens.astype(F32)
    inverse_one = scale_of(source)
    normed_one = source * inverse_one
    source_all = flat(tokens_all.astype(F32))
    normed_all = source_all * scale_of(source_all)
    first_hidden = (normed_all * gain_attn).astype(BF)
    qkv = nn(first_hidden, weight_qkv)
    attended = attend_forward(qkv, tables, seq_count, query_width, key_width)
    middle = source + rows_sum(nt(attended, weight_out))
    inverse_two = scale_of(middle)
    normed_two = middle * inverse_two
    second_hidden = flat(rows_all((normed_two * gain_mlp).astype(BF)))

    gate_value = nn(second_hidden, weight_gate)
    up_projected = nn(second_hidden, weight_up)
    sigmoid_gate = jax.nn.sigmoid(gate_value)
    silu_gate = gate_value * sigmoid_gate
    active = (silu_gate * up_projected).astype(BF)
    active_gradient = nn(cotangent_all, weight_down)
    gate_rows = (
        active_gradient * up_projected * (sigmoid_gate * (1.0 + gate_value * (1.0 - sigmoid_gate)))
    ).astype(BF)
    up_rows = (active_gradient * silu_gate).astype(BF)
    hidden_two_part = nt(gate_rows, weight_gate) + nt(up_rows, weight_up)
    mlp_grads = jnp.concatenate(
        [
            tn(second_hidden, gate_rows).astype(BF),
            tn(second_hidden, up_rows).astype(BF),
            tn(cotangent_all, active).astype(BF),
        ],
        axis=1,
    )
    dsecond, mlp_grads = lax.optimization_barrier((rows_sum(hidden_two_part), mlp_grads))
    mlp_sums = sum_shards(mlp_grads)
    layer_out = (middle + rows_sum(nt(active, weight_down))).astype(BF)

    mlp_gain_part = jnp.sum(dsecond * normed_two, axis=(0, 1))
    shaped = dsecond * gain_mlp
    back_two = inverse_two * (
        shaped - normed_two * jnp.mean(shaped * normed_two, axis=-1, keepdims=True)
    )
    grad_middle = cotangent.astype(F32) + back_two

    attention_gradient = flat(rows_all(grad_middle.astype(BF)))
    grad_mixed = nn(attention_gradient, weight_out).astype(BF)
    query_back, key_back, value_back, head_gains = attend_backward(
        qkv, grad_mixed, tables, seq_count, query_width, key_width
    )
    qkv_back = jnp.concatenate([query_back, key_back, value_back], axis=1)
    hidden_one_part = nt(qkv_back, weight_qkv)
    attn_gain_part = jnp.sum(hidden_one_part * normed_all, axis=0)
    head_gains = jnp.sum(head_gains, axis=(0, 1))

    def spread(vector):
        split = vector.reshape(-1, head_rows)
        return jnp.pad(split, ((0, 0), (0, shard_rows - head_rows))).reshape(-1)

    gain_parts = jnp.stack(
        [attn_gain_part, mlp_gain_part, spread(head_gains[0]), spread(head_gains[1])], axis=1
    )
    attention_grads = jnp.concatenate(
        [
            tn(first_hidden, qkv_back).astype(BF),
            tn(attention_gradient, attended).astype(BF),
            jnp.pad(gain_parts, ((0, 0), (0, LANES - 4))).astype(BF),
        ],
        axis=1,
    )
    attention_grads, mlp_sums = lax.optimization_barrier((attention_grads, mlp_sums))
    attention_sums = sum_shards(attention_grads).astype(F32)
    gain_sums = lax.psum(attention_sums[:, qkv_width + query_width :], "tensor") if (
        n_tensor != 2
    ) else attention_sums[:, qkv_width + query_width :] + lax.ppermute(
        attention_sums[:, qkv_width + query_width :], "tensor", swap
    )

    dhidden = rows_sum(hidden_one_part)
    shaped = dhidden * gain_attn
    back_one = inverse_one * (
        shaped - normed_one * jnp.mean(shaped * normed_one, axis=-1, keepdims=True)
    )
    grad_tokens = grad_middle + back_one
    mlp_sums = mlp_sums.astype(F32)
    return (
        layer_out,
        grad_tokens,
        gain_sums[:, 0],
        gain_sums[:, 1],
        gain_sums[:head_rows, 2],
        gain_sums[:head_rows, 3],
        attention_sums[:, :query_width],
        attention_sums[:, query_width : query_width + key_width],
        attention_sums[:, query_width + key_width : qkv_width],
        attention_sums[:, qkv_width : qkv_width + query_width].T,
        mlp_sums[:, :hidden_units],
        mlp_sums[:, hidden_units : 2 * hidden_units],
        mlp_sums[:, 2 * hidden_units :].T,
    )


def solution(mesh):
    split = P("fsdp", "tensor")
    turned = P("tensor", "fsdp")
    rows = P("fsdp", "tensor", None)
    vector = P("fsdp")
    in_specs = (rows, P("fsdp", None), vector, vector, vector, vector)
    in_specs = in_specs + (split, split, split, turned, split, split, turned, rows)
    out_specs = (rows, rows, vector, vector, vector, vector)
    out_specs = out_specs + (split, split, split, turned, split, split, turned)
    return jax.shard_map(
        functools.partial(local, mesh.shape["tensor"]),
        mesh=mesh,
        in_specs=in_specs,
        out_specs=out_specs,
        check_vma=False,
    )
```

```python
import functools

import jax
import jax.numpy as jnp
from jax import lax
from jax.experimental import pallas as pl
from jax.experimental.pallas import tpu as pltpu
from jax.sharding import PartitionSpec as P

epsilon = 1e-06
rope_base = 1000000.0
LANES = 128
BF = jnp.bfloat16
F32 = jnp.float32


def starts_of(segment_rows):
    seq_length = segment_rows.shape[-1]
    token_index = jnp.arange(seq_length, dtype=jnp.int32)
    change = jnp.concatenate(
        [
            jnp.ones(segment_rows.shape[:-1] + (1,), bool),
            segment_rows[..., 1:] != segment_rows[..., :-1],
        ],
        axis=-1,
    )
    return lax.cummax(jnp.where(change, token_index, 0), axis=segment_rows.ndim - 1)


def rope_tables(positions, width):
    half_width = width // 2
    frequency = rope_base ** (-jnp.arange(half_width, dtype=F32) * 2.0 / width)
    angles = positions.astype(F32)[..., None] * frequency
    cosine_table = jnp.cos(angles)
    sine_table = jnp.sin(angles)
    return (
        jnp.concatenate([cosine_table, cosine_table], -1),
        jnp.concatenate([-sine_table, sine_table], -1),
    )


def scale_of(vector):
    return lax.rsqrt(jnp.mean(vector * vector, axis=-1, keepdims=True) + epsilon)


def nt(left, right):
    return lax.dot_general(left, right, (((1,), (1,)), ((), ())), preferred_element_type=F32)


def nn(left, right):
    return jnp.dot(left, right, preferred_element_type=F32)


def tn(left, right):
    return lax.dot_general(left, right, (((0,), (0,)), ((), ())), preferred_element_type=F32)


def turn(vector):
    return pltpu.roll(vector, vector.shape[1] // 2, 1)


def prepared(raw, gain, cosine, sine):
    inverse = scale_of(raw)
    normed = raw * inverse
    gained = normed * gain
    return (gained * cosine + turn(gained) * sine).astype(BF), normed, inverse


def scores_block(key_part, query_part, starts, key_first, query_first, scale):
    scores = nt(key_part, query_part) * scale
    key_index = lax.broadcasted_iota(jnp.int32, scores.shape, 0) + key_first
    query_index = lax.broadcasted_iota(jnp.int32, scores.shape, 1) + query_first
    allowed = (key_index <= query_index) & (key_index >= starts)
    return jnp.where(allowed, scores, -1000000000.0)


def soft_block(scores):
    exponent = jnp.exp(scores - jnp.max(scores, axis=0, keepdims=True))
    return exponent * (1.0 / jnp.sum(exponent, axis=0, keepdims=True))


def for_windows(begins_ref, block, grain, seq_length, body):
    sequence = pl.program_id(0)
    for first in range(0, seq_length, block):
        tile = begins_ref[sequence, first // block] // grain
        for lower in range(0, first + 1, grain):

            @pl.when(tile == lower // grain)
            def _(lower=lower, first=first):
                body(lower, first, first + block)


def forward_kernel(
    group,
    block,
    grain,
    begins_ref,
    q_ref,
    k_ref,
    v_ref,
    cos_ref,
    sin_ref,
    starts_ref,
    qg_ref,
    kg_ref,
    out_ref,
    key_rot,
    value_turned,
    query_rot,
):
    seq_length, head_dim = k_ref.shape
    scale = head_dim**-0.5
    cosine, sine = cos_ref[...], sin_ref[...]

    @pl.when(pl.program_id(2) == 0)
    def _():
        key_rot[...] = prepared(k_ref[...], kg_ref[...], cosine, sine)[0]
        value_turned[...] = v_ref[...].T.astype(BF)

    query_rot[...] = prepared(q_ref[...], qg_ref[...], cosine, sine)[0]

    def body(lower, first, last):
        scores = scores_block(
            key_rot[lower:last, :],
            query_rot[first:last, :],
            starts_ref[:, first:last],
            lower,
            first,
            scale,
        )
        probs = soft_block(scores).astype(BF)
        out_ref[first:last, :] = nn(value_turned[:, lower:last], probs).T.astype(BF)

    for_windows(begins_ref, block, grain, seq_length, body)


def backward_kernel(
    group,
    block,
    grain,
    begins_ref,
    q_ref,
    k_ref,
    v_ref,
    grad_ref,
    cos_ref,
    sin_ref,
    starts_ref,
    qg_ref,
    kg_ref,
    dq_ref,
    dk_ref,
    dv_ref,
    gains_ref,
    key_total,
    value_total,
    query_total,
    key_rot,
    key_turned,
    value,
    query_rot,
):
    seq_length, head_dim = k_ref.shape
    scale = head_dim**-0.5
    cosine, sine = cos_ref[...], sin_ref[...]
    key_gain, query_gain = kg_ref[...], qg_ref[...]

    @pl.when(pl.program_id(2) == 0)
    def _():
        rotated = prepared(k_ref[...], key_gain, cosine, sine)[0]
        key_rot[...] = rotated
        key_turned[...] = rotated.astype(F32).T.astype(BF)
        value[...] = v_ref[...].astype(BF)
        key_total[...] = jnp.zeros_like(key_total)
        value_total[...] = jnp.zeros_like(value_total)

    query_rotated, query_normed, query_inverse = prepared(q_ref[...], query_gain, cosine, sine)
    query_rot[...] = query_rotated

    def norm_back(rounded, normed, inverse, gain):
        gradient = rounded.astype(BF).astype(F32)
        gradient = gradient * cosine - turn(gradient) * sine
        gain_grad = jnp.sum(gradient * normed, axis=0, keepdims=True)
        shaped = gradient * gain
        inner = jnp.mean(shaped * normed, axis=-1, keepdims=True)
        return (inverse * (shaped - normed * inner)).astype(BF), gain_grad

    def body(lower, first, last):
        query_part = query_rot[first:last, :]
        grad_part = grad_ref[first:last, :]
        probs = soft_block(
            scores_block(
                key_rot[lower:last, :],
                query_part,
                starts_ref[:, first:last],
                lower,
                first,
                scale,
            )
        )
        grad_probs = nt(value[lower:last, :], grad_part)
        delta = jnp.sum(grad_probs * probs, axis=0, keepdims=True)
        score_grad = (probs * (grad_probs - delta)).astype(BF)
        value_total[lower:last, :] += nn(probs.astype(BF), grad_part)
        key_total[lower:last, :] += nn(score_grad, query_part)
        query_total[first:last, :] = nn(key_turned[:, lower:last], score_grad).T

    for_windows(begins_ref, block, grain, seq_length, body)

    query_back, gain_part = norm_back(
        query_total[...] * scale, query_normed, query_inverse, query_gain
    )
    dq_ref[...] = query_back
    gains_ref[0:1, :] = gain_part
    gains_ref[1:2, :] = jnp.zeros_like(gain_part)

    @pl.when(pl.program_id(2) == group - 1)
    def _():
        _, key_normed, key_inverse = prepared(k_ref[...], key_gain, cosine, sine)
        key_back, key_gain_part = norm_back(
            key_total[...] * scale, key_normed, key_inverse, key_gain
        )
        dk_ref[...] = key_back
        dv_ref[...] = value_total[...].astype(BF)
        gains_ref[1:2, :] = key_gain_part


def attention_specs(seq_length, query_width, key_width, head_dim):
    key_heads = key_width // head_dim
    group = query_width // key_width
    key_base = query_width // head_dim
    value_base = key_base + key_heads
    wide = pl.BlockSpec((seq_length, head_dim), lambda s, h, g, b: (s, h * group + g))
    narrow = pl.BlockSpec((seq_length, head_dim), lambda s, h, g, b: (s, h))
    raw = [
        wide,
        pl.BlockSpec((seq_length, head_dim), lambda s, h, g, b: (s, key_base + h)),
        pl.BlockSpec((seq_length, head_dim), lambda s, h, g, b: (s, value_base + h)),
    ]
    tables = [
        pl.BlockSpec((seq_length, head_dim), lambda s, h, g, b: (s, 0)),
        pl.BlockSpec((seq_length, head_dim), lambda s, h, g, b: (s, 0)),
        pl.BlockSpec((None, 1, seq_length), lambda s, h, g, b: (s, 0, 0)),
        pl.BlockSpec((1, head_dim), lambda s, h, g, b: (0, 0)),
        pl.BlockSpec((1, head_dim), lambda s, h, g, b: (0, 0)),
    ]
    return raw, tables, wide, narrow, group, key_heads


def attention_tiles(seq_length):
    return min(256, seq_length), min(128, seq_length)


def attend_forward(qkv, tables, seq_count, query_width, key_width):
    seq_length = qkv.shape[0] // seq_count
    head_dim = tables[0].shape[-1]
    raw_specs, table_specs, wide, _, group, key_heads = attention_specs(
        seq_length, query_width, key_width, head_dim
    )
    block, grain = attention_tiles(seq_length)
    begins = tables[2][:, 0, ::block]
    return pl.pallas_call(
        functools.partial(forward_kernel, group, block, grain),
        grid_spec=pltpu.PrefetchScalarGridSpec(
            num_scalar_prefetch=1,
            grid=(seq_count, key_heads, group),
            in_specs=raw_specs + table_specs,
            out_specs=wide,
            scratch_shapes=[
                pltpu.VMEM((seq_length, head_dim), BF),
                pltpu.VMEM((head_dim, seq_length), BF),
                pltpu.VMEM((seq_length, head_dim), BF),
            ],
        ),
        out_shape=jax.ShapeDtypeStruct((qkv.shape[0], query_width), BF),
        compiler_params=pltpu.CompilerParams(vmem_limit_bytes=32 * 2**20),
        cost_estimate=pl.CostEstimate(
            flops=2 * seq_count * seq_length * seq_length * query_width,
            bytes_accessed=qkv.size * 4 + qkv.shape[0] * query_width * 2,
            transcendentals=seq_count * seq_length * seq_length * query_width // head_dim,
        ),
    )(begins, qkv, qkv, qkv, *tables)


def attend_backward(qkv, grad_mixed, tables, seq_count, query_width, key_width):
    seq_length = qkv.shape[0] // seq_count
    head_dim = tables[0].shape[-1]
    raw_specs, table_specs, wide, narrow, group, key_heads = attention_specs(
        seq_length, query_width, key_width, head_dim
    )
    block, grain = attention_tiles(seq_length)
    begins = tables[2][:, 0, ::block]
    rows = qkv.shape[0]
    total = pltpu.VMEM((seq_length, head_dim), F32)
    part = pltpu.VMEM((seq_length, head_dim), BF)
    return pl.pallas_call(
        functools.partial(backward_kernel, group, block, grain),
        grid_spec=pltpu.PrefetchScalarGridSpec(
            num_scalar_prefetch=1,
            grid=(seq_count, key_heads, group),
            in_specs=raw_specs + [wide] + table_specs,
            out_specs=[
                wide,
                narrow,
                narrow,
                pl.BlockSpec(
                    (None, None, 2, head_dim), lambda s, h, g, b: (s, h * group + g, 0, 0)
                ),
            ],
            scratch_shapes=[total, total, total, part]
            + [pltpu.VMEM((head_dim, seq_length), BF), part, part],
        ),
        out_shape=[
            jax.ShapeDtypeStruct((rows, query_width), BF),
            jax.ShapeDtypeStruct((rows, key_width), BF),
            jax.ShapeDtypeStruct((rows, key_width), BF),
            jax.ShapeDtypeStruct((seq_count, key_heads * group, 2, head_dim), F32),
        ],
        compiler_params=pltpu.CompilerParams(vmem_limit_bytes=32 * 2**20),
        cost_estimate=pl.CostEstimate(
            flops=5 * seq_count * seq_length * seq_length * query_width,
            bytes_accessed=qkv.size * 6 + rows * query_width * 2,
            transcendentals=seq_count * seq_length * seq_length * query_width // head_dim,
        ),
    )(begins, qkv, qkv, qkv, grad_mixed, *tables)


def local(
    n_tensor,
    tokens,
    segments,
    attn_gain,
    mlp_gain,
    query_gain,
    key_gain,
    query_weight,
    key_matrix,
    value_matrix,
    output_weight,
    gate_weight,
    up_weight,
    down_weight,
    cotangent,
):
    seq_count, local_rows, width = tokens.shape
    seq_length = segments.shape[1]
    shard_rows = attn_gain.shape[0]
    head_rows = query_gain.shape[0]
    query_width = query_weight.shape[1]
    key_width = key_matrix.shape[1]
    hidden_units = gate_weight.shape[1]
    qkv_width = query_width + 2 * key_width
    me = lax.axis_index("tensor")
    swap = [(0, 1), (1, 0)]

    def rows_all(member):
        if n_tensor == 2:
            other = lax.ppermute(member, "tensor", swap)
            return jnp.concatenate(
                [jnp.where(me == 0, member, other), jnp.where(me == 0, other, member)], axis=1
            )
        return lax.all_gather(member, "tensor", axis=1, tiled=True)

    def rows_sum(member):
        member = member.reshape(seq_count, seq_length, width)
        if n_tensor == 2:
            lower, upper = member[:, :local_rows], member[:, local_rows:]
            sent = jnp.where(me == 0, upper, lower).astype(BF)
            kept = jnp.where(me == 0, lower, upper)
            return kept + lax.ppermute(sent, "tensor", swap).astype(F32)
        return lax.psum_scatter(member, "tensor", scatter_dimension=1, tiled=True)

    def sum_shards(member):
        return lax.psum_scatter(member, "fsdp", scatter_dimension=0, tiled=True)

    def flat(member):
        return member.reshape(seq_count * seq_length, -1)

    def column(vector):
        return jnp.pad(vector[:, None], ((0, shard_rows - vector.shape[0]), (0, 0)))

    gain_columns = jnp.concatenate(
        [column(member) for member in (attn_gain, mlp_gain, query_gain, key_gain)], axis=1
    )
    gain_columns = jnp.pad(gain_columns, ((0, 0), (0, LANES - 4)))
    first_shard = jnp.concatenate(
        [query_weight, key_matrix, value_matrix, output_weight.T, gain_columns], axis=1
    )
    second_shard = jnp.concatenate([gate_weight, up_weight, down_weight.T], axis=1)
    first_all = lax.all_gather(first_shard, "fsdp", axis=0, tiled=True)
    second_all = lax.all_gather(second_shard, "fsdp", axis=0, tiled=True)
    weight_qkv = first_all[:, :qkv_width]
    weight_out = first_all[:, qkv_width : qkv_width + query_width]
    gains = first_all[:, qkv_width + query_width :].astype(F32)
    gain_attn, gain_mlp = gains[:, 0], gains[:, 1]
    split_gains = gains.reshape(-1, shard_rows, LANES)[:, :head_rows]
    gain_query = split_gains[:, :, 2].reshape(1, -1)
    gain_key = split_gains[:, :, 3].reshape(1, -1)
    weight_gate = second_all[:, :hidden_units]
    weight_up = second_all[:, hidden_units : 2 * hidden_units]
    weight_down = second_all[:, 2 * hidden_units :]
    head_dim = gain_query.shape[1]

    tokens_all, cotangent_all = lax.optimization_barrier((rows_all(tokens), rows_all(cotangent)))
    cotangent_all = flat(cotangent_all)
    starts = starts_of(segments)
    positions = jnp.arange(seq_length, dtype=jnp.int32) - starts
    cosine_table, sine_table = rope_tables(positions, head_dim)
    tables = (
        flat(cosine_table),
        flat(sine_table),
        starts.reshape(seq_count, 1, seq_length),
        gain_query,
        gain_key,
    )

    source = tokens.astype(F32)
    inverse_one = scale_of(source)
    normed_one = source * inverse_one
    source_all = flat(tokens_all.astype(F32))
    normed_all = source_all * scale_of(source_all)
    first_hidden = (normed_all * gain_attn).astype(BF)
    qkv = nn(first_hidden, weight_qkv)
    attended = attend_forward(qkv, tables, seq_count, query_width, key_width)
    middle = source + rows_sum(nt(attended, weight_out))
    inverse_two = scale_of(middle)
    normed_two = middle * inverse_two
    second_hidden = flat(rows_all((normed_two * gain_mlp).astype(BF)))

    gate_value = nn(second_hidden, weight_gate)
    up_projected = nn(second_hidden, weight_up)
    sigmoid_gate = jax.nn.sigmoid(gate_value)
    silu_gate = gate_value * sigmoid_gate
    active = (silu_gate * up_projected).astype(BF)
    active_gradient = nn(cotangent_all, weight_down)
    gate_rows = (
        active_gradient * up_projected * (sigmoid_gate * (1.0 + gate_value * (1.0 - sigmoid_gate)))
    ).astype(BF)
    up_rows = (active_gradient * silu_gate).astype(BF)
    hidden_two_part = nt(gate_rows, weight_gate) + nt(up_rows, weight_up)
    mlp_grads = jnp.concatenate(
        [
            tn(second_hidden, gate_rows).astype(BF),
            tn(second_hidden, up_rows).astype(BF),
            tn(cotangent_all, active).astype(BF),
        ],
        axis=1,
    )
    dsecond, mlp_grads = lax.optimization_barrier((rows_sum(hidden_two_part), mlp_grads))
    mlp_sums = sum_shards(mlp_grads)
    layer_out = (middle + rows_sum(nt(active, weight_down))).astype(BF)

    mlp_gain_part = jnp.sum(dsecond * normed_two, axis=(0, 1))
    shaped = dsecond * gain_mlp
    back_two = inverse_two * (
        shaped - normed_two * jnp.mean(shaped * normed_two, axis=-1, keepdims=True)
    )
    grad_middle = cotangent.astype(F32) + back_two

    attention_gradient = flat(rows_all(grad_middle.astype(BF)))
    grad_mixed = nn(attention_gradient, weight_out).astype(BF)
    query_back, key_back, value_back, head_gains = attend_backward(
        qkv, grad_mixed, tables, seq_count, query_width, key_width
    )
    qkv_back = jnp.concatenate([query_back, key_back, value_back], axis=1)
    hidden_one_part = nt(qkv_back, weight_qkv)
    attn_gain_part = jnp.sum(hidden_one_part * normed_all, axis=0)
    head_gains = jnp.sum(head_gains, axis=(0, 1))

    def spread(vector):
        split = vector.reshape(-1, head_rows)
        return jnp.pad(split, ((0, 0), (0, shard_rows - head_rows))).reshape(-1)

    gain_parts = jnp.stack(
        [attn_gain_part, mlp_gain_part, spread(head_gains[0]), spread(head_gains[1])]
    )
    if n_tensor == 2:
        gain_parts = gain_parts + lax.ppermute(gain_parts, "tensor", swap)
    else:
        gain_parts = lax.psum(gain_parts, "tensor")
    attention_grads = jnp.concatenate(
        [
            tn(first_hidden, qkv_back).astype(BF),
            tn(attention_gradient, attended).astype(BF),
            jnp.pad(gain_parts.T, ((0, 0), (0, LANES - 4))).astype(BF),
        ],
        axis=1,
    )
    attention_grads, mlp_sums = lax.optimization_barrier((attention_grads, mlp_sums))
    attention_sums = sum_shards(attention_grads).astype(F32)
    gain_sums = attention_sums[:, qkv_width + query_width :]

    dhidden = rows_sum(hidden_one_part)
    shaped = dhidden * gain_attn
    back_one = inverse_one * (
        shaped - normed_one * jnp.mean(shaped * normed_one, axis=-1, keepdims=True)
    )
    grad_tokens = grad_middle + back_one
    mlp_sums = mlp_sums.astype(F32)
    return (
        layer_out,
        grad_tokens,
        gain_sums[:, 0],
        gain_sums[:, 1],
        gain_sums[:head_rows, 2],
        gain_sums[:head_rows, 3],
        attention_sums[:, :query_width],
        attention_sums[:, query_width : query_width + key_width],
        attention_sums[:, query_width + key_width : qkv_width],
        attention_sums[:, qkv_width : qkv_width + query_width].T,
        mlp_sums[:, :hidden_units],
        mlp_sums[:, hidden_units : 2 * hidden_units],
        mlp_sums[:, 2 * hidden_units :].T,
    )


def solution(mesh):
    split = P("fsdp", "tensor")
    turned = P("tensor", "fsdp")
    rows = P("fsdp", "tensor", None)
    vector = P("fsdp")
    in_specs = (rows, P("fsdp", None), vector, vector, vector, vector)
    in_specs = in_specs + (split, split, split, turned, split, split, turned, rows)
    out_specs = (rows, rows, vector, vector, vector, vector)
    out_specs = out_specs + (split, split, split, turned, split, split, turned)
    return jax.shard_map(
        functools.partial(local, mesh.shape["tensor"]),
        mesh=mesh,
        in_specs=in_specs,
        out_specs=out_specs,
        check_vma=False,
    )
```
